256 devices in a mesh: row: 4 (over x), col: 4 (over y), gz: 16 (over z, core).
Axes of the slice: x: 4, y: 4, z: 8, core: 2. Of those that a mesh axis runs over, the one named last changes fastest.
Arguments:
- col_panels: bfloat16 [16, 8, 4096, 256], P('gz', 'col', 'row'), may hold values from -0.3984375 to 0.3984375
- row_panels: bfloat16 [16, 8, 256, 4096], P('gz', 'row', None, 'col'), may hold values from -0.796875 to 0.796875
- diag_inverse: bfloat16 [16, 8, 256, 256], P('gz', 'col')
- live: int32 [16], P('gz'), may hold values from 1 to 8, as said below
- schur_block: float32 [4096, 4096], P(('row', 'gz'), 'col'), may hold values from -6 to 6
Outputs:
- updated: float32 [4096, 4096], P(('row', 'gz'), 'col')
The draws below stay inside these ranges and needn't reach their ends.
Inputs may be any that keep to these rules, and one draw needn't show every extreme that they name: Slots 0 to live[z] - 1 of layer z take part; some layer has all 8 slots live.
All inputs are finite; a program needn't handle non-finite values.
Results may differ from the reference program's by a relative error of at most 0.0028.
Values may be sent and summed in bfloat16 or wider, within the bound.
A program may use at most 64 MiB of HBM per device.

```python
import math
import jax
import jax.numpy as jnp
from jax import lax

W = 256
S = 8
NA = 4096
LAYERS = 16


def draw_diag_inverse(key, part):
    key = jax.random.fold_in(key, 7)
    first, second = jax.random.split(key, 2)
    diagonal = jax.random.uniform(first, (LAYERS, S, W), minval=1.5, maxval=3.0)
    offdiag = jax.random.normal(second, (LAYERS, S, W, W)) / math.sqrt(W)
    matrix = jnp.eye(W, dtype=jnp.float32) * diagonal[..., None] + offdiag
    return matrix.astype(jnp.bfloat16)


def draw_live(key, part):
    key = jax.random.fold_in(key, 11)
    first, second = jax.random.split(key)
    counts = jax.random.randint(first, (LAYERS,), 1, S + 1)
    fullest = jax.random.randint(second, (), 0, LAYERS)
    return jnp.where(jnp.arange(LAYERS) == fullest, S, counts).astype(jnp.int32)


def block_levels(key, extent, cuts, smallest, top_value):
    def one(axis_at, shards_of):
        steps = jax.random.uniform(jax.random.fold_in(jax.random.fold_in(key, 6), axis_at), (shards_of,), jnp.float32, smallest / len(cuts), top_value / len(cuts))
        return jnp.repeat(jnp.exp(steps), extent[axis_at] // shards_of).reshape((-1,) + (1,) * (len(extent) - axis_at - 1))

    loudness = one(*cuts[0])
    for cut in cuts[1:]:
        loudness = loudness * one(*cut)
    return loudness


def centred(own_key, extent, scale, most, cuts=(), kind=jnp.bfloat16):
    gain = block_levels(own_key, extent, cuts, -0.22, 0.18) if cuts else 1.0
    entries = jax.random.normal(own_key, extent, jnp.float32) * scale * gain
    return jnp.minimum(jnp.maximum(entries, -most), most).astype(kind)


def setup_inputs(seed: int = 0) -> dict:
    key_of = jax.random.split(jax.random.key(seed), 6)
    col_panels = centred(key_of[0], (LAYERS, S, NA, W), 0.06, 0.3984375, ((0, 16), (1, 4), (2, 4)))
    row_panels = centred(key_of[1], (LAYERS, S, W, NA), 0.12, 0.796875, ((0, 16), (1, 4), (3, 4)))
    diag_inverse = draw_diag_inverse(jax.random.fold_in(key_of[5], 71), 0)
    live = draw_live(jax.random.fold_in(key_of[5], 71), 0)
    schur_block = centred(key_of[4], (NA, NA), 1.0, 6.0, ((0, 64), (1, 4)), jnp.float32)
    return {"col_panels": col_panels, "row_panels": row_panels, "diag_inverse": diag_inverse, "live": live, "schur_block": schur_block}


def reference(col_panels, row_panels, diag_inverse, live, schur_block):
    slot_ids = jnp.arange(col_panels.shape[1])

    def layer_step(total, layer_index):
        lower = jnp.einsum('srw,swv->srv', col_panels[layer_index].astype(jnp.float32), diag_inverse[layer_index].astype(jnp.float32)).astype(jnp.bfloat16)
        keeper = (slot_ids < live[layer_index]).astype(jnp.bfloat16)
        lower = lower * keeper[:, None, None]
        flat_lower = jnp.transpose(lower, (1, 0, 2)).reshape(NA, -1)
        flat_upper = row_panels[layer_index].reshape(-1, NA)
        return total + jnp.dot(flat_lower, flat_upper, preferred_element_type=jnp.float32), None

    total, _ = lax.scan(layer_step, jnp.zeros((NA, NA), jnp.float32), jnp.arange(LAYERS))
    return schur_block - total
```

```python
import functools

import jax
import jax.numpy as jnp
from jax import lax
from jax.experimental import pallas as pl
from jax.experimental.pallas import tpu as pltpu
from jax.sharding import PartitionSpec as P

MESH = pl.DeviceIdType.MESH
F32 = jnp.float32
BF16 = jnp.bfloat16
PARTS = 4
H = 16
CW = 256
CR = 256


def group_blocks():
    groups = []
    for p in range(PARTS):
        blocks = [(i, p) for i in range(p)] + [(p, j) for j in range(p + 1)]
        if len(blocks) > 5:
            groups.append((p, blocks[:4]))
            groups.append((p, blocks[4:]))
        else:
            groups.append((p, blocks))
    return groups


GROUPS = group_blocks()


def kernel(live_ref, x_hbm, u_hbm, d_hbm, out_ref, *scr):
    scr = list(scr)
    xs, dg, lg = scr[:3]
    del scr[:3]
    ug = [scr.pop(0) for _ in range(PARTS)]
    cx = [scr.pop(0) for _ in GROUPS]
    cr = [scr.pop(0) for _ in GROUPS]
    zs = [scr.pop(0) for _ in GROUPS]
    zr = [scr.pop(0) for _ in GROUPS]
    load_sem, ring_send, ring_recv, core_send, core_recv, z_send, z_recv = scr

    r, c, g = lax.axis_index("row"), lax.axis_index("col"), lax.axis_index("gz")
    z, core = lax.div(g, 2), lax.rem(g, 2)

    def along(axis, d):
        if axis == 0:
            return (lax.rem(r + 4 + d, 4), c, g)
        return (r, lax.rem(c + 4 + d, 4), g)

    other_core = (r, c, 2 * z + 1 - core)

    def z_at(d):
        return lax.rem(z + d, 8)

    def z_dev(d):
        return (r, c, 2 * z_at(d) + core)

    loads = [
        pltpu.make_async_copy(d_hbm, dg, load_sem.at[0]),
        pltpu.make_async_copy(x_hbm, xs, load_sem.at[1]),
    ]
    for t in range(PARTS):
        loads.append(
            pltpu.make_async_copy(
                u_hbm.at[:, :, pl.ds(CW * t, CW)],
                ug[t].at[pl.ds(2 * r, 2)],
                load_sem.at[2 + t],
            )
        )
    for cp in loads:
        cp.start()

    barrier = pltpu.get_barrier_semaphore()
    peers = [along(a, d) for a in (0, 1) for d in (1, -1)]
    peers += [other_core] + [z_dev(d) for d in range(1, 8)]
    for dev in peers:
        pl.semaphore_signal(barrier, inc=1, device_id=dev, device_id_type=MESH)

    def lower(t):
        for s in range(2):
            keep = jnp.where(2 * c + s < live_ref[0], 1.0, 0.0).astype(F32)
            halves = [
                xs[s, :, par, H * t : H * t + H, :].reshape(CR // 2, 256)
                for par in range(2)
            ]
            prod = jnp.dot(
                jnp.concatenate(halves, axis=0), dg[s], preferred_element_type=F32
            )
            lg[2 * c + s, CR * t : CR * t + CR, :] = (prod * keep).astype(BF16)

    def piece(axis, slot, t):
        if axis == 0:
            return ug[t].at[slot]
        return lg.at[slot, pl.ds(CR * t, CR)]

    me = (r, c)
    copies = {}

    def ring_copy(axis, t, way, kind):
        key = (axis, t, way, kind)
        if key not in copies:
            d = 1 if way == 0 else -1
            if kind < 2:
                slot = 2 * me[axis] + kind
            else:
                slot = 2 * lax.rem(me[axis] + 4 - d, 4) + way
            sem = ((axis * PARTS + t) * 2 + way) * 3 + kind
            src = dst = piece(axis, slot, t)
            if axis == 0 and kind < 2:
                src = u_hbm.at[kind, :, pl.ds(CW * t, CW)]
            copies[key] = pltpu.make_async_remote_copy(
                src_ref=src,
                dst_ref=dst,
                send_sem=ring_send.at[sem],
                recv_sem=ring_recv.at[sem],
                device_id=along(axis, d),
                device_id_type=MESH,
            )
        return copies[key]

    def direct(axis, t):
        for n in range(2):
            for way in range(2):
                ring_copy(axis, t, way, n if way == 0 else 1 - n).start()

    def forward(t):
        for axis in range(2):
            for way in range(2):
                ring_copy(axis, t, way, way).wait_recv()
                ring_copy(axis, t, way, 2).start()

    def rest(t):
        for axis in range(2):
            for way in range(2):
                ring_copy(axis, t, way, 1 - way).wait_recv()
        for axis in range(2):
            for way in range(2):
                ring_copy(axis, t, way, 2).wait_recv()

    def ring_sent(t):
        for axis in range(2):
            for way in range(2):
                for kind in range(3):
                    ring_copy(axis, t, way, kind).wait_send()

    def core_copy(n, b):
        q = sum(len(blocks) for _, blocks in GROUPS[:n]) + b
        return pltpu.make_async_remote_copy(
            src_ref=cx[n].at[b, 1 - core],
            dst_ref=cr[n].at[b],
            send_sem=core_send.at[q],
            recv_sem=core_recv.at[q],
            device_id=other_core,
            device_id_type=MESH,
        )

    def z_copy(n, d):
        q = 7 * n + d - 1
        return pltpu.make_async_remote_copy(
            src_ref=zs[n].at[z_at(d)],
            dst_ref=zr[n].at[d - 1],
            send_sem=z_send.at[q],
            recv_sem=z_recv.at[q],
            device_id=z_dev(d),
            device_id_type=MESH,
        )

    def multiply(n):
        for b, (i, j) in enumerate(GROUPS[n][1]):
            left = jnp.concatenate(
                [lg[s, CR * i : CR * i + CR, :] for s in range(8)], axis=1
            )
            right = ug[j][...].reshape(2048, CW)
            cx[n][b] = jnp.dot(left, right, preferred_element_type=F32).reshape(
                2, CR // 2, CW
            )
            core_copy(n, b).start()

    def scatter(n):
        for b in range(len(GROUPS[n][1])):
            core_copy(n, b).wait()
            total = cx[n][b, core] + cr[n][b]
            cx[n][b, core] = total
            zs[n][:, H * b : H * b + H, :] = total.reshape(8, H, CW).astype(BF16)
        for d in (4, 3, 5, 2, 6, 1, 7):
            z_copy(n, d).start()

    def finish(n):
        for d in (1, 7, 2, 6, 3, 5, 4):
            z_copy(n, d).wait()
        for b, (i, j) in enumerate(GROUPS[n][1]):
            total = cx[n][b, core, pl.ds(pl.multiple_of(H * z, H), H), :]
            for d in range(1, 8):
                total += zr[n][d - 1, H * b : H * b + H, :].astype(F32)
            out_ref[H * i : H * i + H, CW * j : CW * j + CW] = total

    of_phase = [[n for n, (p, _) in enumerate(GROUPS) if p == q] for q in range(PARTS)]

    loads[0].wait()
    loads[1].wait()
    lower(0)
    pl.semaphore_wait(barrier, len(peers))
    direct(0, 0)
    direct(1, 0)
    direct(0, 1)
    lower(1)
    direct(1, 1)
    for t in range(2, PARTS):
        lower(t)
    for cp in loads[2:]:
        cp.wait()
    for t in range(PARTS + 1):
        if t < PARTS:
            forward(t)
            if t + 2 < PARTS:
                direct(0, t + 2)
                direct(1, t + 2)
        if t >= 2:
            for n in of_phase[t - 2]:
                scatter(n)
        if t >= 1:
            rest(t - 1)
            for n in of_phase[t - 1]:
                multiply(n)
            ring_sent(t - 1)
    for n in of_phase[PARTS - 1]:
        scatter(n)
    for n in range(len(GROUPS)):
        finish(n)


def local(col_panels, row_panels, diag_inverse, live, schur_block):
    panels = col_panels[0].reshape(2, 8, 2, 64, 256)
    count = [len(blocks) for _, blocks in GROUPS]
    any_spec = pl.BlockSpec(memory_space=pl.ANY)
    summed = pl.pallas_call(
        kernel,
        out_shape=jax.ShapeDtypeStruct((64, 1024), F32),
        in_specs=[pl.BlockSpec(memory_space=pltpu.SMEM)] + [any_spec] * 3,
        out_specs=pl.BlockSpec(memory_space=pltpu.VMEM),
        scratch_shapes=[
            pltpu.VMEM((2, 8, 2, 64, 256), BF16),
            pltpu.VMEM((2, 256, 256), BF16),
            pltpu.VMEM((8, 1024, 256), BF16),
        ]
        + [pltpu.VMEM((8, 256, CW), BF16) for _ in range(PARTS)]
        + [pltpu.VMEM((k, 2, CR // 2, CW), F32) for k in count]
        + [pltpu.VMEM((k, CR // 2, CW), F32) for k in count]
        + [pltpu.VMEM((8, H * k, CW), BF16) for k in count]
        + [pltpu.VMEM((7, H * k, CW), BF16) for k in count]
        + [
            pltpu.SemaphoreType.DMA((2 + PARTS,)),
            pltpu.SemaphoreType.DMA((12 * PARTS,)),
            pltpu.SemaphoreType.DMA((12 * PARTS,)),
            pltpu.SemaphoreType.DMA((sum(count),)),
            pltpu.SemaphoreType.DMA((sum(count),)),
            pltpu.SemaphoreType.DMA((7 * len(count),)),
            pltpu.SemaphoreType.DMA((7 * len(count),)),
        ],
        compiler_params=pltpu.CompilerParams(
            collective_id=0, has_side_effects=True, vmem_limit_bytes=56 << 20
        ),
        name="schur_update",
    )(live, panels, row_panels[0], diag_inverse[0])
    return schur_block - summed


def solution(mesh):
    placed = (
        P("gz", "col", "row", None),
        P("gz", "row", None, "col"),
        P("gz", "col", None, None),
        P("gz"),
        P(("row", "gz"), "col"),
    )
    return jax.shard_map(
        local, mesh=mesh, in_specs=placed, out_specs=P(("row", "gz"), "col"), check_vma=False
    )
```

```python
import jax
import jax.numpy as jnp
from jax import lax
from jax.experimental import pallas as pl
from jax.experimental.pallas import tpu as pltpu
from jax.sharding import PartitionSpec as P

MESH = pl.DeviceIdType.MESH
F32 = jnp.float32
BF16 = jnp.bfloat16

HEIGHT = (16, 16, 8, 8, 8, 8)
WIDTH = (256, 256, 128, 128, 128, 128)
PARTS = len(WIDTH)
TOP = tuple(sum(HEIGHT[:t]) for t in range(PARTS))
LEFT = tuple(sum(WIDTH[:t]) for t in range(PARTS))

PRODUCTS = (
    ((0, 1, 0, 1),),
    ((1, 1, 0, 1), (1, 1, 1, 1), (0, 1, 1, 1)),
    ((2, 1, 0, 1), (2, 1, 1, 1), (0, 1, 2, 1), (1, 1, 2, 1)),
    ((3, 1, 0, 1), (3, 1, 1, 1), (0, 1, 3, 1), (1, 1, 3, 1), (2, 2, 2, 1), (2, 2, 3, 1)),
    ((4, 1, 0, 1), (4, 1, 1, 1), (0, 1, 4, 1), (1, 1, 4, 1), (4, 1, 2, 2), (2, 2, 4, 1)),
    ((5, 1, 0, 1), (5, 1, 1, 1), (0, 1, 5, 1), (1, 1, 5, 1)),
    ((5, 1, 2, 2), (2, 2, 5, 1), (4, 2, 4, 1), (4, 2, 5, 1)),
)
PHASE = (0, 1, 2, 3, 4, 5, 5)
GROUPS = len(PRODUCTS)
EARLY = (4, 5, 6)


def units_of(product):
    i, rows, j, columns = product
    row, col = TOP[i], LEFT[j]
    if HEIGHT[i] * rows == 16:
        return [
            ((row, col + k), (row + 8, col + k))
            for k in range(0, WIDTH[j] * columns, 128)
        ]
    return [((row, col), (row, col + 128))]


UNITS = tuple([u for product in group for u in units_of(product)] for group in PRODUCTS)


def first_unit(n, b):
    return sum(len(units_of(product)) for product in PRODUCTS[n][:b])


def kernel(live_ref, x_hbm, u_hbm, d_hbm, out_ref, *scr):
    scr = list(scr)
    xs, dg, lg = scr[:3]
    del scr[:3]
    ug = [scr.pop(0) for _ in range(PARTS)]
    cx = [scr.pop(0) for _ in range(GROUPS)]
    cr = [scr.pop(0) for _ in range(GROUPS)]
    zs = [scr.pop(0) for _ in range(GROUPS)]
    zr = [scr.pop(0) for _ in range(GROUPS)]
    load_sem, ring_send, ring_recv, core_send, core_recv, z_send, z_recv = scr

    r, c, g = lax.axis_index("row"), lax.axis_index("col"), lax.axis_index("gz")
    z, core = lax.div(g, 2), lax.rem(g, 2)
    me = (r, c)

    def along(axis, d):
        if axis == 0:
            return (lax.rem(r + 4 + d, 4), c, g)
        return (r, lax.rem(c + 4 + d, 4), g)

    other_core = (r, c, 2 * z + 1 - core)

    def z_at(d):
        return lax.rem(z + d, 8)

    def z_dev(d):
        return (r, c, 2 * z_at(d) + core)

    barrier = pltpu.get_barrier_semaphore()
    peers = [along(a, d) for a in (0, 1) for d in (1, -1)]
    peers += [other_core] + [z_dev(d) for d in range(1, 8)]
    for dev in peers:
        pl.semaphore_signal(barrier, inc=1, device_id=dev, device_id_type=MESH)

    loads = [
        pltpu.make_async_copy(d_hbm, dg, load_sem.at[0]),
        pltpu.make_async_copy(x_hbm, xs, load_sem.at[1]),
    ]
    for t in range(PARTS):
        loads.append(
            pltpu.make_async_copy(
                u_hbm.at[:, :, pl.ds(LEFT[t], WIDTH[t])],
                ug[t].at[pl.ds(2 * r, 2)],
                load_sem.at[2 + t],
            )
        )
    for cp in loads:
        cp.start()

    def lower(t):
        for s in range(2):
            keep = jnp.where(2 * c + s < live_ref[0], 1.0, 0.0).astype(F32)
            halves = [
                xs[s, :, par, TOP[t] : TOP[t] + 16, :].reshape(128, 256)
                for par in range(2)
            ]
            prod = keep * jnp.dot(
                jnp.concatenate(halves, axis=0), dg[s], preferred_element_type=F32
            )
            slot = 2 * c + s
            if HEIGHT[t] == 16:
                lg[slot, 16 * TOP[t] : 16 * TOP[t] + 256, :] = prod.astype(BF16)
            else:
                prod = prod.reshape(16, 16, 256)
                for k in range(2):
                    at = 16 * TOP[t + k]
                    lg[slot, at : at + 128, :] = (
                        prod[:, 8 * k : 8 * k + 8, :].reshape(128, 256).astype(BF16)
                    )

    def piece(axis, slot, t):
        if axis == 0:
            return ug[t].at[slot]
        return lg.at[slot, pl.ds(16 * TOP[t], 16 * HEIGHT[t])]

    copies = {}

    def ring_copy(axis, t, way, kind):
        key = (axis, t, way, kind)
        if key not in copies:
            d = 1 if way == 0 else -1
            if kind < 2:
                slot = 2 * me[axis] + kind
            else:
                slot = 2 * lax.rem(me[axis] + 4 - d, 4) + way
            sem = ((axis * PARTS + t) * 2 + way) * 3 + kind
            src = dst = piece(axis, slot, t)
            if axis == 0 and kind < 2:
                src = u_hbm.at[kind, :, pl.ds(LEFT[t], WIDTH[t])]
            copies[key] = pltpu.make_async_remote_copy(
                src_ref=src,
                dst_ref=dst,
                send_sem=ring_send.at[sem],
                recv_sem=ring_recv.at[sem],
                device_id=along(axis, d),
                device_id_type=MESH,
            )
        return copies[key]

    def first(axis, t):
        for way in range(2):
            ring_copy(axis, t, way, way).start()

    def second(axis, t):
        for way in range(2):
            ring_copy(axis, t, way, 1 - way).start()

    def forward(t):
        for axis in range(2):
            for way in range(2):
                ring_copy(axis, t, way, way).wait_recv()
                ring_copy(axis, t, way, 2).start()
        for axis in range(2):
            if t + 1 < PARTS:
                second(axis, t + 1)
            if t + 2 < PARTS:
                first(axis, t + 2)

    def neighbours(t):
        for axis in range(2):
            for way in range(2):
                ring_copy(axis, t, way, 1 - way).wait_recv()

    def rest(t):
        if PHASE.index(t) not in EARLY:
            neighbours(t)
        for axis in range(2):
            for way in range(2):
                ring_copy(axis, t, way, 2).wait_recv()

    def ring_sent(t):
        for axis in range(2):
            for way in range(2):
                for kind in range(3):
                    ring_copy(axis, t, way, kind).wait_send()

    def core_copy(n, b):
        q = sum(len(group) for group in PRODUCTS[:n]) + b
        at = pl.ds(first_unit(n, b), len(units_of(PRODUCTS[n][b])))
        return pltpu.make_async_remote_copy(
            src_ref=cx[n].at[1 - core, at],
            dst_ref=cr[n].at[at],
            send_sem=core_send.at[q],
            recv_sem=core_recv.at[q],
            device_id=other_core,
            device_id_type=MESH,
        )

    def z_copy(n, d):
        q = 7 * n + d - 1
        return pltpu.make_async_remote_copy(
            src_ref=zs[n].at[z_at(d)],
            dst_ref=zr[n].at[d - 1],
            send_sem=z_send.at[q],
            recv_sem=z_recv.at[q],
            device_id=z_dev(d),
            device_id_type=MESH,
        )

    def factors(product, slots):
        i, many, j, columns = product
        rows = pl.ds(16 * TOP[i], 16 * HEIGHT[i] * many)
        left = jnp.concatenate([lg[s, rows, :] for s in slots], axis=1)
        right = [
            jnp.concatenate([ug[k][s] for s in slots], axis=0)
            for k in range(j, j + columns)
        ]
        return left, right[0] if columns == 1 else jnp.concatenate(right, axis=1)

    def by_units(product, prod):
        i, many, j, columns = product
        width = WIDTH[j] * columns
        if many == 2:
            prod = prod.reshape(2, 2, 8, 8, 128)
            return [jnp.concatenate([prod[0], prod[1]], axis=2)]
        if HEIGHT[i] == 16:
            prod = prod.reshape(2, 8, 16, width)
            return [prod[..., k : k + 128] for k in range(0, width, 128)]
        prod = prod.reshape(2, 8, 8, width)
        return [jnp.concatenate([prod[..., 0:128], prod[..., 128:256]], axis=2)]

    def slots_of(n, product, far):
        i, many, j, columns = product
        late = i + many - 1 == PHASE[n], j + columns - 1 == PHASE[n]
        if all(late):
            return None
        at = me[1] if late[0] else me[0]
        steps = (2,) if far else (0, 1, 3)
        return [2 * lax.rem(at + d, 4) + s for d in steps for s in range(2)]

    def begin(n):
        for b, product in enumerate(PRODUCTS[n]):
            slots = slots_of(n, product, False)
            if slots is not None:
                prod = jnp.dot(*factors(product, slots), preferred_element_type=F32)
                for k, unit in enumerate(by_units(product, prod)):
                    cx[n][:, first_unit(n, b) + k] = unit

    def multiply(n):
        for b, product in enumerate(PRODUCTS[n]):
            slots = slots_of(n, product, True) if n in EARLY else None
            prod = jnp.dot(
                *factors(product, range(8) if slots is None else slots),
                preferred_element_type=F32,
            )
            for k, unit in enumerate(by_units(product, prod)):
                u = first_unit(n, b) + k
                if slots is not None:
                    unit += cx[n][:, u]
                cx[n][:, u] = unit
            core_copy(n, b).start()

    def add_cores(n):
        for b in range(len(PRODUCTS[n])):
            core_copy(n, b).wait()
        for u in range(len(UNITS[n])):
            total = cx[n][core, u] + cr[n][u]
            cx[n][core, u] = total
            zs[n][:, 16 * u : 16 * u + 16, :] = total.astype(BF16)

    def scatter(n):
        add_cores(n)
        for d in (4, 3, 5, 2, 6, 1, 7):
            z_copy(n, d).start()

    def write(unit, total):
        for k, (row, col) in enumerate(unit):
            out_ref[row : row + 8, col : col + 128] = total[8 * k : 8 * k + 8, :]

    def finish(n):
        for d in (1, 7, 2, 6, 3, 5, 4):
            z_copy(n, d).wait()
        for u, unit in enumerate(UNITS[n]):
            total = cx[n][core, u, z]
            for d in range(1, 8):
                total += zr[n][d - 1, 16 * u : 16 * u + 16, :].astype(F32)
            write(unit, total)

    loads[0].wait()
    loads[1].wait()
    lower(0)
    lower(1)
    pl.semaphore_wait(barrier, len(peers))
    for axis in range(2):
        first(axis, 0)
    for axis in range(2):
        second(axis, 0)
    for axis in range(2):
        first(axis, 1)
    lower(2)
    lower(4)
    for cp in loads[2:]:
        cp.wait()

    forward(0)
    forward(1)
    rest(0)
    multiply(0)
    forward(2)
    scatter(0)
    ring_sent(0)
    rest(1)
    multiply(1)
    forward(3)
    scatter(1)
    rest(2)
    multiply(2)
    forward(4)
    scatter(2)
    ring_sent(1)
    rest(3)
    multiply(3)
    forward(5)
    neighbours(4)
    begin(4)
    scatter(3)
    rest(4)
    multiply(4)
    neighbours(5)
    begin(5)
    begin(6)
    scatter(4)
    rest(5)
    multiply(5)
    multiply(6)
    ring_sent(2)
    scatter(5)
    scatter(6)
    for t in range(3, PARTS):
        ring_sent(t)
    for n in range(GROUPS):
        finish(n)


def local(col_panels, row_panels, diag_inverse, live, schur_block):
    panels = col_panels[0].reshape(2, 8, 2, 64, 256)
    count = [len(units) for units in UNITS]
    products = sum(len(group) for group in PRODUCTS)
    hbm = pl.BlockSpec(memory_space=pltpu.HBM)

    summed = pl.pallas_call(
        kernel,
        out_shape=jax.ShapeDtypeStruct((64, 1024), F32),
        in_specs=[pl.BlockSpec(memory_space=pltpu.SMEM)] + [hbm] * 3,
        out_specs=pl.BlockSpec(memory_space=pltpu.VMEM),
        scratch_shapes=[
            pltpu.VMEM((2, 8, 2, 64, 256), BF16),
            pltpu.VMEM((2, 256, 256), BF16),
            pltpu.VMEM((8, 1024, 256), BF16),
        ]
        + [pltpu.VMEM((8, 256, w), BF16) for w in WIDTH]
        + [pltpu.VMEM((2, k, 8, 16, 128), F32) for k in count]
        + [pltpu.VMEM((k, 8, 16, 128), F32) for k in count]
        + [pltpu.VMEM((8, 16 * k, 128), BF16) for k in count]
        + [pltpu.VMEM((7, 16 * k, 128), BF16) for k in count]
        + [
            pltpu.SemaphoreType.DMA((2 + PARTS,)),
            pltpu.SemaphoreType.DMA((12 * PARTS,)),
            pltpu.SemaphoreType.DMA((12 * PARTS,)),
            pltpu.SemaphoreType.DMA((products,)),
            pltpu.SemaphoreType.DMA((products,)),
            pltpu.SemaphoreType.DMA((7 * GROUPS,)),
            pltpu.SemaphoreType.DMA((7 * GROUPS,)),
        ],
        compiler_params=pltpu.CompilerParams(
            collective_id=0, has_side_effects=True, vmem_limit_bytes=53 << 20
        ),
        name="schur_update",
    )(live, panels, row_panels[0], diag_inverse[0])
    return schur_block - summed


def solution(mesh):
    placed = (
        P("gz", "col", "row", None),
        P("gz", "row", None, "col"),
        P("gz", "col", None, None),
        P("gz"),
        P(("row", "gz"), "col"),
    )
    return jax.shard_map(
        local, mesh=mesh, in_specs=placed, out_specs=P(("row", "gz"), "col"), check_vma=False
    )
```

```python
import jax
import jax.numpy as jnp
from jax import lax
from jax.experimental import pallas as pl
from jax.experimental.pallas import tpu as pltpu
from jax.sharding import PartitionSpec as P

MESH = pl.DeviceIdType.MESH
F32 = jnp.float32
BF16 = jnp.bfloat16

HEIGHT = (16, 16, 8, 8, 8, 8)
WIDTH = (256, 256, 128, 128, 128, 128)
PARTS = len(WIDTH)
TOP = tuple(sum(HEIGHT[:t]) for t in range(PARTS))
LEFT = tuple(sum(WIDTH[:t]) for t in range(PARTS))

PRODUCTS = (
    ((0, 1, 0, 1),),
    ((1, 1, 0, 1), (1, 1, 1, 1), (0, 1, 1, 1)),
    ((2, 1, 0, 1), (2, 1, 1, 1), (0, 1, 2, 1), (1, 1, 2, 1)),
    ((3, 1, 0, 1), (3, 1, 1, 1), (0, 1, 3, 1), (1, 1, 3, 1), (2, 2, 2, 1), (2, 2, 3, 1)),
    ((4, 1, 0, 1), (4, 1, 1, 1), (0, 1, 4, 1), (1, 1, 4, 1), (4, 1, 2, 2), (2, 2, 4, 1)),
    ((5, 1, 0, 1), (5, 1, 1, 1), (0, 1, 5, 1), (1, 1, 5, 1), (5, 1, 2, 2), (2, 2, 5, 1), (4, 2, 4, 1), (4, 2, 5, 1)),
)
PHASE = (0, 1, 2, 3, 4, 5)
GROUPS = len(PRODUCTS)
RELAYED = (3, 4, 5)
EARLY = (4, 5)


def units_of(product):
    i, rows, j, columns = product
    row, col = TOP[i], LEFT[j]
    if HEIGHT[i] * rows == 16:
        return [
            ((row, col + k), (row + 8, col + k))
            for k in range(0, WIDTH[j] * columns, 128)
        ]
    return [((row, col), (row, col + 128))]


UNITS = tuple([u for product in group for u in units_of(product)] for group in PRODUCTS)


def first_unit(n, b):
    return sum(len(units_of(product)) for product in PRODUCTS[n][:b])


def kernel(live_ref, x_hbm, u_hbm, d_hbm, out_ref, *scr):
    scr = list(scr)
    xs, dg, lg = scr[:3]
    del scr[:3]
    ug = [scr.pop(0) for _ in range(PARTS)]
    cx = [scr.pop(0) for _ in range(GROUPS)]
    cr = [scr.pop(0) for _ in range(GROUPS)]
    zs = [scr.pop(0) for _ in range(GROUPS)]
    zr = [scr.pop(0) for _ in range(GROUPS)]
    load_sem, ring_send, ring_recv, core_send, core_recv, z_send, z_recv = scr

    r, c, g = lax.axis_index("row"), lax.axis_index("col"), lax.axis_index("gz")
    z, core = lax.div(g, 2), lax.rem(g, 2)
    me = (r, c)

    def along(axis, d):
        if axis == 0:
            return (lax.rem(r + 4 + d, 4), c, g)
        return (r, lax.rem(c + 4 + d, 4), g)

    other_core = (r, c, 2 * z + 1 - core)

    def z_at(d):
        return lax.rem(z + d, 8)

    def z_dev(d):
        return (r, c, 2 * z_at(d) + core)

    def load(n, src, dst):
        return pltpu.make_async_copy(src, dst, load_sem.at[n])

    load_d = load(0, d_hbm, dg)
    load_x = [
        load(1 + k, x_hbm.at[:, :, :, pl.ds(16 * k, 16)], xs.at[:, :, :, pl.ds(16 * k, 16)])
        for k in range(4)
    ]
    load_u = [
        load(5 + t, u_hbm.at[:, :, pl.ds(LEFT[t], WIDTH[t])], ug[t].at[pl.ds(2 * r, 2)])
        for t in range(PARTS)
    ]
    load_d.start()
    load_x[0].start()

    barrier = pltpu.get_barrier_semaphore()
    peers = [along(a, d) for a in (0, 1) for d in (1, -1)]
    peers += [other_core] + [z_dev(d) for d in range(1, 8)]
    for dev in peers:
        pl.semaphore_signal(barrier, inc=1, device_id=dev, device_id_type=MESH)
    for cp in load_x[1:] + load_u:
        cp.start()

    def lower(t):
        load_x[TOP[t] // 16].wait()
        for s in range(2):
            keep = jnp.where(2 * c + s < live_ref[0], 1.0, 0.0).astype(F32)
            halves = [
                xs[s, :, par, TOP[t] : TOP[t] + 16, :].reshape(128, 256)
                for par in range(2)
            ]
            prod = keep * jnp.dot(
                jnp.concatenate(halves, axis=0), dg[s], preferred_element_type=F32
            )
            slot = 2 * c + s
            if HEIGHT[t] == 16:
                lg[slot, 16 * TOP[t] : 16 * TOP[t] + 256, :] = prod.astype(BF16)
            else:
                prod = prod.reshape(16, 16, 256)
                for k in range(2):
                    at = 16 * TOP[t + k]
                    lg[slot, at : at + 128, :] = (
                        prod[:, 8 * k : 8 * k + 8, :].reshape(128, 256).astype(BF16)
                    )

    def piece(axis, slot, t):
        if axis == 0:
            return ug[t].at[slot]
        return lg.at[slot, pl.ds(16 * TOP[t], 16 * HEIGHT[t])]

    copies = {}

    def ring_copy(axis, t, way, kind):
        key = (axis, t, way, kind)
        if key not in copies:
            d = 1 if way == 0 else -1
            if kind < 2:
                slot = 2 * me[axis] + kind
            else:
                slot = 2 * lax.rem(me[axis] + 4 - d, 4) + way
            sem = ((axis * PARTS + t) * 2 + way) * 3 + kind
            src = dst = piece(axis, slot, t)
            if axis == 0 and kind < 2:
                src = u_hbm.at[kind, :, pl.ds(LEFT[t], WIDTH[t])]
            copies[key] = pltpu.make_async_remote_copy(
                src_ref=src,
                dst_ref=dst,
                send_sem=ring_send.at[sem],
                recv_sem=ring_recv.at[sem],
                device_id=along(axis, d),
                device_id_type=MESH,
            )
        return copies[key]

    def first(axis, t):
        for way in range(2):
            ring_copy(axis, t, way, way).start()

    def second(axis, t):
        for way in range(2):
            ring_copy(axis, t, way, 1 - way).start()

    def forward(t):
        for axis in range(2):
            for way in range(2):
                ring_copy(axis, t, way, way).wait_recv()
        if t == PARTS - 3:
            for axis in range(2):
                first(axis, PARTS - 1)
        for axis in range(2):
            for way in range(2):
                ring_copy(axis, t, way, 2).start()
        for axis in range(2):
            if t + 1 < PARTS:
                second(axis, t + 1)
            if t + 2 < PARTS - 1:
                first(axis, t + 2)

    def neighbours(t):
        for axis in range(2):
            for way in range(2):
                ring_copy(axis, t, way, 1 - way).wait_recv()

    def rest(t):
        if PHASE.index(t) not in EARLY:
            neighbours(t)
        for axis in range(2):
            for way in range(2):
                ring_copy(axis, t, way, 2).wait_recv()

    def ring_sent(t):
        for axis in range(2):
            for way in range(2):
                for kind in range(3):
                    ring_copy(axis, t, way, kind).wait_send()

    def core_copy(n, b):
        q = sum(len(group) for group in PRODUCTS[:n]) + b
        at = pl.ds(first_unit(n, b), len(units_of(PRODUCTS[n][b])))
        return pltpu.make_async_remote_copy(
            src_ref=cx[n].at[1 - core, at],
            dst_ref=cr[n].at[at],
            send_sem=core_send.at[q],
            recv_sem=core_recv.at[q],
            device_id=other_core,
            device_id_type=MESH,
        )

    def z_copy(n, m):
        rows = 16 * len(UNITS[n])
        at = pl.ds(0, rows)
        to = of = m
        if n in RELAYED:
            kind, way = m // 2, m % 2
            to, of = (1, 2, 1, 2)[kind], (3, 4, 1, 2)[kind]
            if way:
                to, of = 8 - to, 8 - of
            if kind == 1:
                at = pl.ds(rows // 2 * way, rows // 2)
        return pltpu.make_async_remote_copy(
            src_ref=zs[n].at[z_at(of), at],
            dst_ref=zr[n].at[m, at],
            send_sem=z_send.at[8 * n + m],
            recv_sem=z_recv.at[8 * n + m],
            device_id=z_dev(to),
            device_id_type=MESH,
        )

    def factors(product, slots):
        i, many, j, columns = product
        rows = pl.ds(16 * TOP[i], 16 * HEIGHT[i] * many)
        left = jnp.concatenate([lg[s, rows, :] for s in slots], axis=1)
        right = [
            jnp.concatenate([ug[k][s] for s in slots], axis=0)
            for k in range(j, j + columns)
        ]
        return left, right[0] if columns == 1 else jnp.concatenate(right, axis=1)

    def by_units(product, prod):
        i, many, j, columns = product
        width = WIDTH[j] * columns
        if many == 2:
            prod = prod.reshape(2, 2, 8, 8, 128)
            return [jnp.concatenate([prod[0], prod[1]], axis=2)]
        if HEIGHT[i] == 16:
            prod = prod.reshape(2, 8, 16, width)
            return [prod[..., k : k + 128] for k in range(0, width, 128)]
        prod = prod.reshape(2, 8, 8, width)
        return [jnp.concatenate([prod[..., 0:128], prod[..., 128:256]], axis=2)]

    def slots_of(n, product, far):
        i, many, j, columns = product
        late = i + many - 1 == PHASE[n], j + columns - 1 == PHASE[n]
        if all(late):
            return None
        at = me[1] if late[0] else me[0]
        steps = (2,) if far else (0, 1, 3)
        return [2 * lax.rem(at + d, 4) + s for d in steps for s in range(2)]

    def begin(n):
        for b, product in enumerate(PRODUCTS[n]):
            slots = slots_of(n, product, False)
            if slots is not None:
                prod = jnp.dot(*factors(product, slots), preferred_element_type=F32)
                for k, unit in enumerate(by_units(product, prod)):
                    cx[n][:, first_unit(n, b) + k] = unit

    def multiply(n):
        for b, product in enumerate(PRODUCTS[n]):
            slots = slots_of(n, product, True) if n in EARLY else None
            prod = jnp.dot(
                *factors(product, range(8) if slots is None else slots),
                preferred_element_type=F32,
            )
            for k, unit in enumerate(by_units(product, prod)):
                u = first_unit(n, b) + k
                if slots is not None:
                    unit += cx[n][:, u]
                cx[n][:, u] = unit
            core_copy(n, b).start()

    def add_cores(n):
        for b in range(len(PRODUCTS[n])):
            core_copy(n, b).wait()
        for u in range(len(UNITS[n])):
            total = cx[n][core, u] + cr[n][u]
            cx[n][core, u] = total
            zs[n][:, 16 * u : 16 * u + 16, :] = total.astype(BF16)

    def scatter(n):
        add_cores(n)
        for m in (2, 3, 0, 1, 4, 5) if n in RELAYED else (4, 3, 5, 2, 6, 1, 7):
            z_copy(n, m).start()

    def relay(n):
        rows = 16 * len(UNITS[n])
        for way in range(2):
            z_copy(n, way).wait()
            z_copy(n, 2 + way).wait()
            dest = z_at(6 if way else 2)
            total = cx[n][core, :, dest].reshape(rows, 128) + zr[n][way].astype(F32)
            half = [slice(0, rows // 2), slice(rows // 2, rows)]
            mine, other = half[way], half[1 - way]
            more = zr[n][2 + way, mine, :].astype(F32)
            zs[n][dest, mine, :] = (total[mine] + more).astype(BF16)
            zs[n][dest, other, :] = total[other].astype(BF16)
            z_copy(n, 6 + way).start()

    def write(unit, total):
        for k, (row, col) in enumerate(unit):
            out_ref[row : row + 8, col : col + 128] = total[8 * k : 8 * k + 8, :]

    def finish(n):
        last = (4, 5, 6, 7) if n in RELAYED else (1, 7, 2, 6, 3, 5, 4)
        for m in last:
            z_copy(n, m).wait()
        for u, unit in enumerate(UNITS[n]):
            total = cx[n][core, u, z]
            for m in last:
                total += zr[n][m, 16 * u : 16 * u + 16, :].astype(F32)
            write(unit, total)

    load_d.wait()
    lower(0)
    lower(1)
    pl.semaphore_wait(barrier, len(peers))
    for axis in (1, 0):
        first(axis, 0)
    for axis in (1, 0):
        second(axis, 0)
    for axis in (1, 0):
        first(axis, 1)
    lower(2)
    lower(4)
    for cp in load_u:
        cp.wait()

    forward(0)
    forward(1)
    rest(0)
    multiply(0)
    forward(2)
    scatter(0)
    ring_sent(0)
    rest(1)
    multiply(1)
    forward(3)
    scatter(1)
    rest(2)
    multiply(2)
    forward(4)
    scatter(2)
    ring_sent(1)
    forward(5)
    rest(3)
    multiply(3)
    neighbours(4)
    begin(4)
    scatter(3)
    rest(4)
    multiply(4)
    neighbours(5)
    begin(5)
    scatter(4)
    rest(5)
    multiply(5)
    relay(3)
    ring_sent(2)
    scatter(5)
    relay(4)
    for t in range(3, PARTS):
        ring_sent(t)
    for n in range(3):
        finish(n)
    relay(5)
    for n in range(3, GROUPS):
        finish(n)


def local(col_panels, row_panels, diag_inverse, live, schur_block):
    panels = col_panels[0].reshape(2, 8, 2, 64, 256)
    operands = panels, row_panels[0], diag_inverse[0]
    count = [len(units) for units in UNITS]
    products = sum(len(group) for group in PRODUCTS)
    hbm = pl.BlockSpec(memory_space=pltpu.HBM)

    summed = pl.pallas_call(
        kernel,
        out_shape=jax.ShapeDtypeStruct((64, 1024), F32),
        in_specs=[pl.BlockSpec(memory_space=pltpu.SMEM)] + [hbm] * 3,
        out_specs=pl.BlockSpec(memory_space=pltpu.VMEM),
        scratch_shapes=[
            pltpu.VMEM((2, 8, 2, 64, 256), BF16),
            pltpu.VMEM((2, 256, 256), BF16),
            pltpu.VMEM((8, 1024, 256), BF16),
        ]
        + [pltpu.VMEM((8, 256, w), BF16) for w in WIDTH]
        + [pltpu.VMEM((2, k, 8, 16, 128), F32) for k in count]
        + [pltpu.VMEM((k, 8, 16, 128), F32) for k in count]
        + [pltpu.VMEM((8, 16 * k, 128), BF16) for k in count]
        + [pltpu.VMEM((8, 16 * k, 128), BF16) for k in count]
        + [
            pltpu.SemaphoreType.DMA((5 + PARTS,)),
            pltpu.SemaphoreType.DMA((12 * PARTS,)),
            pltpu.SemaphoreType.DMA((12 * PARTS,)),
            pltpu.SemaphoreType.DMA((products,)),
            pltpu.SemaphoreType.DMA((products,)),
            pltpu.SemaphoreType.DMA((8 * GROUPS,)),
            pltpu.SemaphoreType.DMA((8 * GROUPS,)),
        ],
        compiler_params=pltpu.CompilerParams(
            collective_id=0, has_side_effects=True, vmem_limit_bytes=40 << 20
        ),
        name="schur_update",
    )(live, *[pltpu.with_memory_space_constraint(a, pltpu.HBM) for a in operands])
    return schur_block - summed


def solution(mesh):
    placed = (
        P("gz", "col", "row", None),
        P("gz", "row", None, "col"),
        P("gz", "col", None, None),
        P("gz"),
        P(("row", "gz"), "col"),
    )
    return jax.shard_map(
        local, mesh=mesh, in_specs=placed, out_specs=P(("row", "gz"), "col"), check_vma=False
    )
```

```python
import jax
import jax.numpy as jnp
from jax import lax
from jax.experimental import pallas as pl
from jax.experimental.pallas import tpu as pltpu
from jax.sharding import PartitionSpec as P

MESH = pl.DeviceIdType.MESH
F32 = jnp.float32
BF16 = jnp.bfloat16

HEIGHT = (32, 8, 8, 8, 8)
WIDTH = (512, 128, 128, 128, 128)
PARTS = len(WIDTH)
TOP = tuple(sum(HEIGHT[:t]) for t in range(PARTS))
LEFT = tuple(sum(WIDTH[:t]) for t in range(PARTS))

PRODUCTS = (
    ((0, 1, 0, 1),),
    ((1, 1, 0, 1), (0, 1, 1, 1)),
    ((2, 1, 0, 1), (0, 1, 2, 1), (1, 2, 1, 1), (1, 2, 2, 1)),
    ((3, 1, 0, 1), (0, 1, 3, 1), (3, 1, 1, 2), (1, 2, 3, 1)),
    ((4, 1, 0, 1), (0, 1, 4, 1), (4, 1, 1, 2), (1, 2, 4, 1), (3, 2, 3, 1), (3, 2, 4, 1)),
)
PHASE = (0, 1, 2, 3, 4)
GROUPS = len(PRODUCTS)
RELAYED = (3, 4)
EARLY = (3, 4)


def units_of(product):
    i, rows, j, columns = product
    row, col, width = TOP[i], LEFT[j], WIDTH[j] * columns
    height = HEIGHT[i] * rows
    if height == 8:
        return [((row, col + k), (row, col + k + 128)) for k in range(0, width, 256)]
    return [
        ((row + a, col + k), (row + a + 8, col + k))
        for a in range(0, height, 16)
        for k in range(0, width, 128)
    ]


UNITS = tuple([u for product in group for u in units_of(product)] for group in PRODUCTS)


def first_unit(n, b):
    return sum(len(units_of(product)) for product in PRODUCTS[n][:b])


def kernel(live_ref, x_hbm, u_hbm, d_hbm, out_ref, *scr):
    scr = list(scr)
    xs, dg, lg = scr[:3]
    del scr[:3]
    ug = [scr.pop(0) for _ in range(PARTS)]
    cx = [scr.pop(0) for _ in range(GROUPS)]
    cr = [scr.pop(0) for _ in range(GROUPS)]
    zs = [scr.pop(0) for _ in range(GROUPS)]
    zr = [scr.pop(0) for _ in range(GROUPS)]
    load_sem, ring_send, ring_recv, core_send, core_recv, z_send, z_recv = scr

    r, c, g = lax.axis_index("row"), lax.axis_index("col"), lax.axis_index("gz")
    z, core = lax.div(g, 2), lax.rem(g, 2)
    me = (r, c)

    def along(axis, d):
        if axis == 0:
            return (lax.rem(r + 4 + d, 4), c, g)
        return (r, lax.rem(c + 4 + d, 4), g)

    other_core = (r, c, 2 * z + 1 - core)

    def z_at(d):
        return lax.rem(z + d, 8)

    def z_dev(d):
        return (r, c, 2 * z_at(d) + core)

    def load(n, src, dst):
        return pltpu.make_async_copy(src, dst, load_sem.at[n])

    load_d = load(0, d_hbm, dg)
    load_x = [
        load(1 + k, x_hbm.at[:, :, :, pl.ds(16 * k, 16)], xs.at[:, :, :, pl.ds(16 * k, 16)])
        for k in range(4)
    ]
    load_u = [
        load(5 + t, u_hbm.at[:, :, pl.ds(LEFT[t], WIDTH[t])], ug[t].at[pl.ds(2 * r, 2)])
        for t in range(PARTS)
    ]
    load_d.start()
    load_x[0].start()

    barrier = pltpu.get_barrier_semaphore()
    peers = [along(a, d) for a in (0, 1) for d in (1, -1)]
    peers += [other_core] + [z_dev(d) for d in range(1, 8)]
    for dev in peers:
        pl.semaphore_signal(barrier, inc=1, device_id=dev, device_id_type=MESH)
    for cp in load_x[1:] + load_u:
        cp.start()

    def lower(t):
        tall = max(HEIGHT[t], 16)
        for k in range(TOP[t] // 16, (TOP[t] + tall) // 16):
            load_x[k].wait()
        for s in range(2):
            keep = jnp.where(2 * c + s < live_ref[0], 1.0, 0.0).astype(F32)
            halves = [
                xs[s, :, par, TOP[t] : TOP[t] + tall, :].reshape(8 * tall, 256)
                for par in range(2)
            ]
            prod = keep * jnp.dot(
                jnp.concatenate(halves, axis=0), dg[s], preferred_element_type=F32
            )
            slot = 2 * c + s
            if HEIGHT[t] == tall:
                lg[slot, 16 * TOP[t] : 16 * (TOP[t] + tall), :] = prod.astype(BF16)
            else:
                prod = prod.reshape(16, 16, 256)
                for k in range(2):
                    at = 16 * TOP[t + k]
                    lg[slot, at : at + 128, :] = (
                        prod[:, 8 * k : 8 * k + 8, :].reshape(128, 256).astype(BF16)
                    )

    def piece(axis, slot, t):
        if axis == 0:
            return ug[t].at[slot]
        return lg.at[slot, pl.ds(16 * TOP[t], 16 * HEIGHT[t])]

    copies = {}

    def ring_copy(axis, t, way, kind):
        key = (axis, t, way, kind)
        if key not in copies:
            d = 1 if way == 0 else -1
            if kind < 2:
                slot = 2 * me[axis] + kind
            else:
                slot = 2 * lax.rem(me[axis] + 4 - d, 4) + way
            sem = ((axis * PARTS + t) * 2 + way) * 3 + kind
            src = dst = piece(axis, slot, t)
            if axis == 0 and kind < 2:
                src = u_hbm.at[kind, :, pl.ds(LEFT[t], WIDTH[t])]
            copies[key] = pltpu.make_async_remote_copy(
                src_ref=src,
                dst_ref=dst,
                send_sem=ring_send.at[sem],
                recv_sem=ring_recv.at[sem],
                device_id=along(axis, d),
                device_id_type=MESH,
            )
        return copies[key]

    def first(axis, t):
        for way in range(2):
            ring_copy(axis, t, way, way).start()

    def second(axis, t):
        for way in range(2):
            ring_copy(axis, t, way, 1 - way).start()

    def forward(t):
        for axis in range(2):
            for way in range(2):
                ring_copy(axis, t, way, way).wait_recv()
                if t == PARTS - 3:
                    ring_copy(axis, PARTS - 1, way, way).start()
                ring_copy(axis, t, way, 2).start()
                if t + 1 < PARTS:
                    ring_copy(axis, t + 1, way, 1 - way).start()
                if t + 2 < PARTS - 1:
                    ring_copy(axis, t + 2, way, way).start()

    def neighbours(t):
        for axis in range(2):
            for way in range(2):
                ring_copy(axis, t, way, 1 - way).wait_recv()

    def rest(t):
        if PHASE.index(t) not in EARLY:
            neighbours(t)
        for axis in range(2):
            for way in range(2):
                ring_copy(axis, t, way, 2).wait_recv()

    def ring_sent(t):
        for axis in range(2):
            for way in range(2):
                for kind in range(3):
                    ring_copy(axis, t, way, kind).wait_send()

    def core_copy(n, b):
        q = sum(len(group) for group in PRODUCTS[:n]) + b
        at = pl.ds(first_unit(n, b), len(units_of(PRODUCTS[n][b])))
        return pltpu.make_async_remote_copy(
            src_ref=cx[n].at[1 - core, at],
            dst_ref=cr[n].at[at],
            send_sem=core_send.at[q],
            recv_sem=core_recv.at[q],
            device_id=other_core,
            device_id_type=MESH,
        )

    def z_copy(n, m):
        rows = 16 * len(UNITS[n])
        at = pl.ds(0, rows)
        to = of = m
        if n in RELAYED:
            kind, way = m // 2, m % 2
            to, of = (1, 2, 1, 2)[kind], (3, 4, 1, 2)[kind]
            if way:
                to, of = 8 - to, 8 - of
            if kind == 1:
                at = pl.ds(rows // 2 * way, rows // 2)
        return pltpu.make_async_remote_copy(
            src_ref=zs[n].at[z_at(of), at],
            dst_ref=zr[n].at[m, at],
            send_sem=z_send.at[8 * n + m],
            recv_sem=z_recv.at[8 * n + m],
            device_id=z_dev(to),
            device_id_type=MESH,
        )

    def factors(product, slots):
        i, many, j, columns = product
        rows = pl.ds(16 * TOP[i], 16 * HEIGHT[i] * many)
        left = jnp.concatenate([lg[s, rows, :] for s in slots], axis=1)
        right = [
            jnp.concatenate([ug[k][s] for s in slots], axis=0)
            for k in range(j, j + columns)
        ]
        return left, right[0] if columns == 1 else jnp.concatenate(right, axis=1)

    def by_units(product, prod):
        i, many, j, columns = product
        width = WIDTH[j] * columns
        if many == 2:
            prod = prod.reshape(2, 2, 8, 8, 128)
            return [jnp.concatenate([prod[0], prod[1]], axis=2)]
        height = HEIGHT[i]
        prod = prod.reshape(2, 8, height, width)
        if height == 8:
            return [
                jnp.concatenate([prod[..., k : k + 128], prod[..., k + 128 : k + 256]], axis=2)
                for k in range(0, width, 256)
            ]
        return [
            prod[:, :, a : a + 16, k : k + 128]
            for a in range(0, height, 16)
            for k in range(0, width, 128)
        ]

    def slots_of(n, product, far):
        i, many, j, columns = product
        late = i + many - 1 == PHASE[n], j + columns - 1 == PHASE[n]
        if all(late):
            return None
        at = me[1] if late[0] else me[0]
        steps = (2,) if far else (0, 1, 3)
        return [2 * lax.rem(at + d, 4) + s for d in steps for s in range(2)]

    def begin(n):
        for b, product in enumerate(PRODUCTS[n]):
            slots = slots_of(n, product, False)
            if slots is not None:
                prod = jnp.dot(*factors(product, slots), preferred_element_type=F32)
                for k, unit in enumerate(by_units(product, prod)):
                    cx[n][:, first_unit(n, b) + k] = unit

    def multiply(n):
        for b, product in enumerate(PRODUCTS[n]):
            slots = slots_of(n, product, True) if n in EARLY else None
            prod = jnp.dot(
                *factors(product, range(8) if slots is None else slots),
                preferred_element_type=F32,
            )
            for k, unit in enumerate(by_units(product, prod)):
                u = first_unit(n, b) + k
                if slots is not None:
                    unit += cx[n][:, u]
                cx[n][:, u] = unit
            core_copy(n, b).start()

    def add_cores(n):
        for b in range(len(PRODUCTS[n])):
            core_copy(n, b).wait()
        for u in range(len(UNITS[n])):
            total = cx[n][core, u] + cr[n][u]
            cx[n][core, u] = total
            zs[n][:, 16 * u : 16 * u + 16, :] = total.astype(BF16)

    def scatter(n):
        add_cores(n)
        for m in (2, 3, 0, 1, 4, 5) if n in RELAYED else (4, 3, 5, 2, 6, 1, 7):
            z_copy(n, m).start()

    def relay(n):
        rows = 16 * len(UNITS[n])
        for way in range(2):
            z_copy(n, way).wait()
            z_copy(n, 2 + way).wait()
            dest = z_at(6 if way else 2)
            total = cx[n][core, :, dest].reshape(rows, 128) + zr[n][way].astype(F32)
            half = [slice(0, rows // 2), slice(rows // 2, rows)]
            mine, other = half[way], half[1 - way]
            more = zr[n][2 + way, mine, :].astype(F32)
            zs[n][dest, mine, :] = (total[mine] + more).astype(BF16)
            zs[n][dest, other, :] = total[other].astype(BF16)
            z_copy(n, 6 + way).start()

    def write(unit, total):
        for k, (row, col) in enumerate(unit):
            out_ref[row : row + 8, col : col + 128] = total[8 * k : 8 * k + 8, :]

    def finish(n):
        last = (4, 5, 6, 7) if n in RELAYED else (1, 7, 2, 6, 3, 5, 4)
        for m in last:
            z_copy(n, m).wait()
        for u, unit in enumerate(UNITS[n]):
            total = cx[n][core, u, z]
            for m in last:
                total += zr[n][m, 16 * u : 16 * u + 16, :].astype(F32)
            write(unit, total)

    load_d.wait()
    lower(0)
    lower(1)
    pl.semaphore_wait(barrier, len(peers))
    for axis in (1, 0):
        first(axis, 0)
    for axis in (1, 0):
        second(axis, 0)
    for axis in (1, 0):
        first(axis, 1)
    lower(3)
    for cp in load_u:
        cp.wait()

    forward(0)
    forward(1)
    rest(0)
    multiply(0)
    forward(2)
    scatter(0)
    rest(1)
    multiply(1)
    forward(3)
    scatter(1)
    ring_sent(0)
    forward(4)
    rest(2)
    multiply(2)
    neighbours(3)
    begin(3)
    scatter(2)
    rest(3)
    multiply(3)
    neighbours(4)
    begin(4)
    scatter(3)
    rest(4)
    multiply(4)
    ring_sent(1)
    scatter(4)
    relay(3)
    for t in range(2, PARTS):
        ring_sent(t)
    for n in range(3):
        finish(n)
    relay(4)
    for n in range(3, GROUPS):
        finish(n)


def local(col_panels, row_panels, diag_inverse, live, schur_block):
    panels = col_panels[0].reshape(2, 8, 2, 64, 256)
    operands = panels, row_panels[0], diag_inverse[0]
    count = [len(units) for units in UNITS]
    products = sum(len(group) for group in PRODUCTS)
    hbm = pl.BlockSpec(memory_space=pltpu.HBM)

    summed = pl.pallas_call(
        kernel,
        out_shape=jax.ShapeDtypeStruct((64, 1024), F32),
        in_specs=[pl.BlockSpec(memory_space=pltpu.SMEM)] + [hbm] * 3,
        out_specs=pl.BlockSpec(memory_space=pltpu.VMEM),
        scratch_shapes=[
            pltpu.VMEM((2, 8, 2, 64, 256), BF16),
            pltpu.VMEM((2, 256, 256), BF16),
            pltpu.VMEM((8, 1024, 256), BF16),
        ]
        + [pltpu.VMEM((8, 256, w), BF16) for w in WIDTH]
        + [pltpu.VMEM((2, k, 8, 16, 128), F32) for k in count]
        + [pltpu.VMEM((k, 8, 16, 128), F32) for k in count]
        + [pltpu.VMEM((8, 16 * k, 128), BF16) for k in count]
        + [pltpu.VMEM((8, 16 * k, 128), BF16) for k in count]
        + [
            pltpu.SemaphoreType.DMA((5 + PARTS,)),
            pltpu.SemaphoreType.DMA((12 * PARTS,)),
            pltpu.SemaphoreType.DMA((12 * PARTS,)),
            pltpu.SemaphoreType.DMA((products,)),
            pltpu.SemaphoreType.DMA((products,)),
            pltpu.SemaphoreType.DMA((8 * GROUPS,)),
            pltpu.SemaphoreType.DMA((8 * GROUPS,)),
        ],
        compiler_params=pltpu.CompilerParams(
            collective_id=0, has_side_effects=True, vmem_limit_bytes=40 << 20
        ),
        name="schur_update",
    )(live, *[pltpu.with_memory_space_constraint(a, pltpu.HBM) for a in operands])
    return schur_block - summed


def solution(mesh):
    placed = (
        P("gz", "col", "row", None),
        P("gz", "row", None, "col"),
        P("gz", "col", None, None),
        P("gz"),
        P(("row", "gz"), "col"),
    )
    return jax.shard_map(
        local, mesh=mesh, in_specs=placed, out_specs=P(("row", "gz"), "col"), check_vma=False
    )
```

```python
import jax
import jax.numpy as jnp
from jax import lax
from jax.experimental import pallas as pl
from jax.experimental.pallas import tpu as pltpu
from jax.sharding import PartitionSpec as P

MESH = pl.DeviceIdType.MESH
F32 = jnp.float32
BF16 = jnp.bfloat16

HEIGHT = (32, 16, 8, 8)
WIDTH = (512, 256, 128, 128)
PARTS = len(WIDTH)
TOP = tuple(sum(HEIGHT[:t]) for t in range(PARTS))
LEFT = tuple(sum(WIDTH[:t]) for t in range(PARTS))

PRODUCTS = (
    ((0, 1, 0, 1),),
    ((1, 1, 0, 1), (0, 1, 1, 1), (1, 1, 1, 1)),
    ((2, 1, 0, 1), (0, 1, 2, 1), (2, 1, 1, 1), (1, 1, 2, 1)),
    ((3, 1, 0, 1), (0, 1, 3, 1), (3, 1, 1, 1), (1, 1, 3, 1), (2, 2, 2, 1), (2, 2, 3, 1)),
)
PHASE = (0, 1, 2, 3)
GROUPS = len(PRODUCTS)
RELAYED = (1, 2, 3)
EARLY = (1, 2, 3)


def units_of(product):
    i, rows, j, columns = product
    row, col, width = TOP[i], LEFT[j], WIDTH[j] * columns
    height = HEIGHT[i] * rows
    if height == 8:
        return [((row, col + k), (row, col + k + 128)) for k in range(0, width, 256)]
    return [
        ((row + a, col + k), (row + a + 8, col + k))
        for a in range(0, height, 16)
        for k in range(0, width, 128)
    ]


UNITS = tuple([u for product in group for u in units_of(product)] for group in PRODUCTS)


def first_unit(n, b):
    return sum(len(units_of(product)) for product in PRODUCTS[n][:b])


def kernel(live_ref, x_hbm, u_hbm, d_hbm, out_ref, *scr):
    scr = list(scr)
    xs, dg, lg = scr[:3]
    del scr[:3]
    ug = [scr.pop(0) for _ in range(PARTS)]
    cx = [scr.pop(0) for _ in range(GROUPS)]
    cr = [scr.pop(0) for _ in range(GROUPS)]
    zs = [scr.pop(0) for _ in range(GROUPS)]
    zr = [scr.pop(0) for _ in range(GROUPS)]
    load_sem, ring_send, ring_recv, core_send, core_recv, z_send, z_recv = scr

    r, c, g = lax.axis_index("row"), lax.axis_index("col"), lax.axis_index("gz")
    z, core = lax.div(g, 2), lax.rem(g, 2)
    me = (r, c)

    def along(axis, d):
        if axis == 0:
            return (lax.rem(r + 4 + d, 4), c, g)
        return (r, lax.rem(c + 4 + d, 4), g)

    other_core = (r, c, 2 * z + 1 - core)

    def z_at(d):
        return lax.rem(z + d, 8)

    def z_dev(d):
        return (r, c, 2 * z_at(d) + core)

    def load(n, src, dst):
        return pltpu.make_async_copy(src, dst, load_sem.at[n])

    load_d = load(0, d_hbm, dg)
    load_x = [
        load(1 + k, x_hbm.at[:, :, :, pl.ds(16 * k, 16)], xs.at[:, :, :, pl.ds(16 * k, 16)])
        for k in range(4)
    ]
    load_u = [
        load(5 + t, u_hbm.at[:, :, pl.ds(LEFT[t], WIDTH[t])], ug[t].at[pl.ds(2 * r, 2)])
        for t in range(PARTS)
    ]
    load_d.start()
    load_x[0].start()

    barrier = pltpu.get_barrier_semaphore()
    peers = [along(a, d) for a in (0, 1) for d in (1, -1)]
    peers += [other_core] + [z_dev(d) for d in range(1, 8)]
    for dev in peers:
        pl.semaphore_signal(barrier, inc=1, device_id=dev, device_id_type=MESH)
    for cp in load_x[1:] + load_u:
        cp.start()

    def lower(t):
        tall = max(HEIGHT[t], 16)
        for k in range(TOP[t] // 16, (TOP[t] + tall) // 16):
            load_x[k].wait()
        for s in range(2):
            keep = jnp.where(2 * c + s < live_ref[0], 1.0, 0.0).astype(F32)
            halves = [
                xs[s, :, par, TOP[t] : TOP[t] + tall, :].reshape(8 * tall, 256)
                for par in range(2)
            ]
            prod = keep * jnp.dot(
                jnp.concatenate(halves, axis=0), dg[s], preferred_element_type=F32
            )
            slot = 2 * c + s
            if HEIGHT[t] == tall:
                lg[slot, 16 * TOP[t] : 16 * (TOP[t] + tall), :] = prod.astype(BF16)
            else:
                prod = prod.reshape(16, 16, 256)
                for k in range(2):
                    at = 16 * TOP[t + k]
                    lg[slot, at : at + 128, :] = (
                        prod[:, 8 * k : 8 * k + 8, :].reshape(128, 256).astype(BF16)
                    )

    def piece(axis, slot, t):
        if axis == 0:
            return ug[t].at[slot]
        return lg.at[slot, pl.ds(16 * TOP[t], 16 * HEIGHT[t])]

    copies = {}

    def ring_copy(axis, t, way, kind):
        key = (axis, t, way, kind)
        if key not in copies:
            d = 1 if way == 0 else -1
            if kind < 2:
                slot = 2 * me[axis] + kind
            else:
                slot = 2 * lax.rem(me[axis] + 4 - d, 4) + way
            sem = ((axis * PARTS + t) * 2 + way) * 3 + kind
            src = dst = piece(axis, slot, t)
            if axis == 0 and kind < 2:
                src = u_hbm.at[kind, :, pl.ds(LEFT[t], WIDTH[t])]
            copies[key] = pltpu.make_async_remote_copy(
                src_ref=src,
                dst_ref=dst,
                send_sem=ring_send.at[sem],
                recv_sem=ring_recv.at[sem],
                device_id=along(axis, d),
                device_id_type=MESH,
            )
        return copies[key]

    def first(axis, t):
        for way in range(2):
            ring_copy(axis, t, way, way).start()

    def second(axis, t):
        for way in range(2):
            ring_copy(axis, t, way, 1 - way).start()

    def forward(t):
        for axis in range(2):
            for way in range(2):
                ring_copy(axis, t, way, way).wait_recv()
                ring_copy(axis, t, way, 2).start()
                if t == PARTS - 3:
                    ring_copy(axis, PARTS - 1, way, way).start()
                if t + 1 < PARTS:
                    ring_copy(axis, t + 1, way, 1 - way).start()
                if t + 2 < PARTS - 1:
                    ring_copy(axis, t + 2, way, way).start()

    def neighbours(t):
        for axis in range(2):
            for way in range(2):
                ring_copy(axis, t, way, 1 - way).wait_recv()

    def rest(t):
        if PHASE.index(t) not in EARLY:
            neighbours(t)
        for axis in range(2):
            for way in range(2):
                ring_copy(axis, t, way, 2).wait_recv()

    def ring_sent(t):
        for axis in range(2):
            for way in range(2):
                for kind in range(3):
                    ring_copy(axis, t, way, kind).wait_send()

    def core_copy(n, b):
        q = sum(len(group) for group in PRODUCTS[:n]) + b
        at = pl.ds(first_unit(n, b), len(units_of(PRODUCTS[n][b])))
        return pltpu.make_async_remote_copy(
            src_ref=cx[n].at[1 - core, at],
            dst_ref=cr[n].at[at],
            send_sem=core_send.at[q],
            recv_sem=core_recv.at[q],
            device_id=other_core,
            device_id_type=MESH,
        )

    def z_copy(n, m):
        rows = 16 * len(UNITS[n])
        at = pl.ds(0, rows)
        to = of = m
        if n in RELAYED:
            kind, way = m // 2, m % 2
            to, of = (1, 2, 1, 2)[kind], (3, 4, 1, 2)[kind]
            if way:
                to, of = 8 - to, 8 - of
            if kind == 1:
                at = pl.ds(rows // 2 * way, rows // 2)
        return pltpu.make_async_remote_copy(
            src_ref=zs[n].at[z_at(of), at],
            dst_ref=zr[n].at[m, at],
            send_sem=z_send.at[8 * n + m],
            recv_sem=z_recv.at[8 * n + m],
            device_id=z_dev(to),
            device_id_type=MESH,
        )

    def factors(product, slots):
        i, many, j, columns = product
        rows = pl.ds(16 * TOP[i], 16 * HEIGHT[i] * many)
        left = jnp.concatenate([lg[s, rows, :] for s in slots], axis=1)
        right = [
            jnp.concatenate([ug[k][s] for s in slots], axis=0)
            for k in range(j, j + columns)
        ]
        return left, right[0] if columns == 1 else jnp.concatenate(right, axis=1)

    def by_units(product, prod):
        i, many, j, columns = product
        width = WIDTH[j] * columns
        if many == 2:
            prod = prod.reshape(2, 2, 8, 8, 128)
            return [jnp.concatenate([prod[0], prod[1]], axis=2)]
        height = HEIGHT[i]
        prod = prod.reshape(2, 8, height, width)
        if height == 8:
            return [
                jnp.concatenate([prod[..., k : k + 128], prod[..., k + 128 : k + 256]], axis=2)
                for k in range(0, width, 256)
            ]
        return [
            prod[:, :, a : a + 16, k : k + 128]
            for a in range(0, height, 16)
            for k in range(0, width, 128)
        ]

    def slots_of(n, product, far):
        i, many, j, columns = product
        late = i + many - 1 == PHASE[n], j + columns - 1 == PHASE[n]
        if all(late):
            return None
        at = me[1] if late[0] else me[0]
        steps = (2,) if far else (0, 1, 3)
        return [2 * lax.rem(at + d, 4) + s for d in steps for s in range(2)]

    def begin(n):
        for b, product in enumerate(PRODUCTS[n]):
            slots = slots_of(n, product, False)
            if slots is not None:
                prod = jnp.dot(*factors(product, slots), preferred_element_type=F32)
                for k, unit in enumerate(by_units(product, prod)):
                    cx[n][:, first_unit(n, b) + k] = unit

    def multiply(n):
        for b, product in enumerate(PRODUCTS[n]):
            slots = slots_of(n, product, True) if n in EARLY else None
            prod = jnp.dot(
                *factors(product, range(8) if slots is None else slots),
                preferred_element_type=F32,
            )
            for k, unit in enumerate(by_units(product, prod)):
                u = first_unit(n, b) + k
                if slots is not None:
                    unit += cx[n][:, u]
                cx[n][:, u] = unit
            core_copy(n, b).start()

    def add_cores(n):
        for b in range(len(PRODUCTS[n])):
            core_copy(n, b).wait()
        for u in range(len(UNITS[n])):
            total = cx[n][core, u] + cr[n][u]
            cx[n][core, u] = total
            zs[n][:, 16 * u : 16 * u + 16, :] = total.astype(BF16)

    def scatter(n):
        add_cores(n)
        for m in (2, 3, 0, 1, 4, 5) if n in RELAYED else (4, 3, 5, 2, 6, 1, 7):
            z_copy(n, m).start()

    def relay(n):
        rows = 16 * len(UNITS[n])
        for way in range(2):
            z_copy(n, way).wait()
            z_copy(n, 2 + way).wait()
            dest = z_at(6 if way else 2)
            total = cx[n][core, :, dest].reshape(rows, 128) + zr[n][way].astype(F32)
            half = [slice(0, rows // 2), slice(rows // 2, rows)]
            mine, other = half[way], half[1 - way]
            more = zr[n][2 + way, mine, :].astype(F32)
            zs[n][dest, mine, :] = (total[mine] + more).astype(BF16)
            zs[n][dest, other, :] = total[other].astype(BF16)
            z_copy(n, 6 + way).start()

    def write(unit, total):
        for k, (row, col) in enumerate(unit):
            out_ref[row : row + 8, col : col + 128] = total[8 * k : 8 * k + 8, :]

    def finish(n):
        last = (4, 5, 6, 7) if n in RELAYED else (1, 7, 2, 6, 3, 5, 4)
        for m in last:
            z_copy(n, m).wait()
        for u, unit in enumerate(UNITS[n]):
            total = cx[n][core, u, z]
            for m in last:
                total += zr[n][m, 16 * u : 16 * u + 16, :].astype(F32)
            write(unit, total)

    load_d.wait()
    lower(0)
    lower(1)
    pl.semaphore_wait(barrier, len(peers))
    for axis in (1, 0):
        first(axis, 0)
    for axis in (1, 0):
        second(axis, 0)
    for axis in (1, 0):
        first(axis, 1)
    lower(2)
    for cp in load_u:
        cp.wait()

    forward(0)
    forward(1)
    rest(0)
    multiply(0)
    neighbours(1)
    begin(1)
    scatter(0)
    forward(2)
    rest(1)
    multiply(1)
    forward(3)
    ring_sent(0)
    neighbours(2)
    begin(2)
    scatter(1)
    rest(2)
    multiply(2)
    neighbours(3)
    begin(3)
    scatter(2)
    rest(3)
    multiply(3)
    relay(1)
    ring_sent(1)
    scatter(3)
    relay(2)
    for t in range(2, PARTS):
        ring_sent(t)
    finish(0)
    finish(1)
    relay(3)
    finish(2)
    finish(3)


def local(col_panels, row_panels, diag_inverse, live, schur_block):
    panels = col_panels[0].reshape(2, 8, 2, 64, 256)
    operands = panels, row_panels[0], diag_inverse[0]
    count = [len(units) for units in UNITS]
    products = sum(len(group) for group in PRODUCTS)
    hbm = pl.BlockSpec(memory_space=pltpu.HBM)

    summed = pl.pallas_call(
        kernel,
        out_shape=jax.ShapeDtypeStruct((64, 1024), F32),
        in_specs=[pl.BlockSpec(memory_space=pltpu.SMEM)] + [hbm] * 3,
        out_specs=pl.BlockSpec(memory_space=pltpu.VMEM),
        scratch_shapes=[
            pltpu.VMEM((2, 8, 2, 64, 256), BF16),
            pltpu.VMEM((2, 256, 256), BF16),
            pltpu.VMEM((8, 1024, 256), BF16),
        ]
        + [pltpu.VMEM((8, 256, w), BF16) for w in WIDTH]
        + [pltpu.VMEM((2, k, 8, 16, 128), F32) for k in count]
        + [pltpu.VMEM((k, 8, 16, 128), F32) for k in count]
        + [pltpu.VMEM((8, 16 * k, 128), BF16) for k in count]
        + [pltpu.VMEM((8, 16 * k, 128), BF16) for k in count]
        + [
            pltpu.SemaphoreType.DMA((5 + PARTS,)),
            pltpu.SemaphoreType.DMA((12 * PARTS,)),
            pltpu.SemaphoreType.DMA((12 * PARTS,)),
            pltpu.SemaphoreType.DMA((products,)),
            pltpu.SemaphoreType.DMA((products,)),
            pltpu.SemaphoreType.DMA((8 * GROUPS,)),
            pltpu.SemaphoreType.DMA((8 * GROUPS,)),
        ],
        compiler_params=pltpu.CompilerParams(
            collective_id=0, has_side_effects=True, vmem_limit_bytes=40 << 20
        ),
        name="schur_update",
    )(live, *[pltpu.with_memory_space_constraint(a, pltpu.HBM) for a in operands])
    return schur_block - summed


def solution(mesh):
    placed = (
        P("gz", "col", "row", None),
        P("gz", "row", None, "col"),
        P("gz", "col", None, None),
        P("gz"),
        P(("row", "gz"), "col"),
    )
    return jax.shard_map(
        local, mesh=mesh, in_specs=placed, out_specs=P(("row", "gz"), "col"), check_vma=False
    )
```
